128 devices in a mesh: blk: 32 (over x, z, y_hi), xor: 4 (over y_lo, core).
Axes of the slice: x: 4, y: 4 (y_hi: 2, y_lo: 2; y = y_hi * 2 + y_lo), z: 4, core: 2. Of those that a mesh axis runs over, the one named last changes fastest.
Arguments:
- users: float32 [131072, 256], P(('blk', 'xor')), may hold values from -1.5 to 1.5
- user_accum: float32 [131072, 256], P(('blk', 'xor')), may hold values from 0.05 to 1
- items: float32 [65536, 256], P(('blk', 'xor')), may hold values from -1.5 to 1.5
- item_accum: float32 [65536, 256], P(('blk', 'xor')), may hold values from 0.05 to 1
- seen_user: int32 [6, 2048], P(None, ('blk', 'xor')), may hold values from 0 to 7
- seen_item: int32 [6, 2048], P(None, ('blk', 'xor')), may hold values from 0 to 3
- row_live: int32 [6, 2048, 128], P(None, ('blk', 'xor')), may hold values 0 or 1
- col_live: int32 [6, 2048, 128], P(None, ('blk', 'xor')), may hold values 0 or 1
- neg_user: int32 [6, 1024], P(None, ('blk', 'xor')), may hold values from 0 to 7
- neg_item: int32 [6, 1024], P(None, ('blk', 'xor')), may hold values from 0 to 3
Outputs:
- users_out: float32 [131072, 256], P(('blk', 'xor'))
- user_accum_out: float32 [131072, 256], P(('blk', 'xor'))
- items_out: float32 [65536, 256], P(('blk', 'xor'))
- item_accum_out: float32 [65536, 256], P(('blk', 'xor'))
The draws below stay inside these ranges and needn't reach their ends.
All inputs are finite; a program needn't handle non-finite values. No bound on the sum of `row_live` or of `col_live` on one device may be relied on, other than what follows from the above.
Results may differ from the reference program's by a relative error of at most 0.0051.
Values sent between devices are 32-bit elements; how exact they have to be, the bound alone decides.
No kernel may reach another device: no remote copies, remote signals or barrier semaphores. Data moves between devices by JAX's collectives and lax.ppermute only.
A program may use at most 64 MiB of HBM per device.

```python
import math
import jax
import jax.numpy as jnp
import numpy as np
from jax import lax

K = 256
TILE = 128
SUBS = 6
USER_DEV = 1024
ITEM_DEV = 512
OBS = 16
NEG = 8
HALF = 256
UT = 8
IT = 4
USERS = 131072
ITEMS = 65536
OBS_ALL = 2048
NEG_ALL = 1024
N_BLK = 32
N_XOR = 4


def touch_ends(entries, key, low, largest):
    longest = entries.shape.index(max(entries.shape))
    spots = []
    for shift in (0, 1):
        where = [jax.random.randint(jax.random.fold_in(key, axis), (), 0, length) for axis, length in enumerate(entries.shape)]
        where[longest] = (where[longest] + shift) % entries.shape[longest]
        spots.append(tuple(where))
    return entries.at[spots[0]].set(low).at[spots[1]].set(largest)


def levels(key, shape, split, low, high):
    def one(position, shards_of):
        steps = jax.random.uniform(jax.random.fold_in(jax.random.fold_in(key, 6), position), (shards_of,), jnp.float32, low / len(split), high / len(split))
        return jnp.repeat(jnp.exp(steps), shape[position] // shards_of).reshape((-1,) + (1,) * (len(shape) - position - 1))

    level = one(*split[0])
    for cut in split[1:]:
        level = level * one(*cut)
    return level


def bell_draw(rng, extent, deviation, most, shards=(), kind=jnp.bfloat16):
    drawn = jax.random.normal(rng, extent, jnp.float32) * deviation
    if len(shards) > 0:
        drawn = levels(rng, extent, shards, -0.22, 0.18) * drawn
    return jnp.clip(drawn, min=-most, max=most).astype(kind)


def setup_inputs(seed: int = 0) -> dict:
    streams_of = jax.random.split(jax.random.key(seed), 11)
    users = bell_draw(streams_of[0], (USERS, K), 0.25, 1.5, ((0, 128),), jnp.float32)
    user_accum = jnp.clip(jnp.exp(math.log(1.0) - 2.9957323 * jax.random.uniform(streams_of[1], (USERS, K), jnp.float32) ** levels(streams_of[1], (USERS, K), ((0, 128),), -0.2, 0.2)), 0.05, 1.0)
    items = bell_draw(streams_of[2], (ITEMS, K), 0.25, 1.5, ((0, 128),), jnp.float32)
    item_accum = jnp.clip(jnp.exp(math.log(1.0) - 2.9957323 * jax.random.uniform(streams_of[3], (ITEMS, K), jnp.float32) ** levels(streams_of[3], (ITEMS, K), ((0, 128),), -0.2, 0.2)), 0.05, 1.0)
    seen_user = touch_ends(jax.random.randint(streams_of[4], (SUBS, OBS_ALL), 0, UT), jax.random.fold_in(streams_of[4], 1), 0, UT - 1).astype(jnp.int32)
    seen_item = touch_ends(jax.random.randint(streams_of[5], (SUBS, OBS_ALL), 0, IT), jax.random.fold_in(streams_of[5], 1), 0, IT - 1).astype(jnp.int32)
    row_live = touch_ends((jax.random.randint(streams_of[6], (SUBS, OBS_ALL, TILE), 0, 4) < 3).astype(jnp.int32), jax.random.fold_in(streams_of[6], 1), 0, 1)
    col_live = touch_ends((jax.random.randint(streams_of[7], (SUBS, OBS_ALL, TILE), 0, 2) < 1).astype(jnp.int32), jax.random.fold_in(streams_of[7], 1), 0, 1)
    neg_user = touch_ends(jax.random.randint(streams_of[8], (SUBS, NEG_ALL), 0, UT), jax.random.fold_in(streams_of[8], 1), 0, UT - 1).astype(jnp.int32)
    neg_item = touch_ends(jax.random.randint(streams_of[9], (SUBS, NEG_ALL), 0, IT), jax.random.fold_in(streams_of[9], 1), 0, IT - 1).astype(jnp.int32)
    return dict(users=users, user_accum=user_accum, items=items, item_accum=item_accum, seen_user=seen_user, seen_item=seen_item, row_live=row_live, col_live=col_live, neg_user=neg_user, neg_item=neg_item)


LEARN_RATE = 0.05
DECAY = 0.02
NEG_WEIGHT = 0.25

def local_step(users, user_accum, items, item_accum, seen_user, seen_item, row_live, col_live, neg_user, neg_item):
    width = users.shape[1]
    user_bf = users.astype(jnp.bfloat16).reshape(-1, 128, width)
    item_bf = items.astype(jnp.bfloat16).reshape(-1, 128, width)
    tile_user = jnp.concatenate([seen_user, neg_user]).astype(jnp.int32)
    tile_item = jnp.concatenate([seen_item, neg_item]).astype(jnp.int32)
    user_tiles = user_bf[tile_user].astype(jnp.float32)
    item_tiles = item_bf[tile_item].astype(jnp.float32)
    observed = row_live.astype(jnp.float32)[:, :, None] * col_live.astype(jnp.float32)[:, None, :]
    negative = jnp.full((neg_user.shape[0], 128, 128), NEG_WEIGHT, jnp.float32)
    weight = jnp.concatenate([observed, negative])
    target = jnp.concatenate([jnp.ones((seen_user.shape[0], 1, 1), jnp.float32), jnp.zeros((neg_user.shape[0], 1, 1), jnp.float32)])
    scores = jnp.einsum('tik,tjk->tij', user_tiles, item_tiles)
    residual = (weight * (scores - target)).astype(jnp.bfloat16).astype(jnp.float32)
    user_terms = jnp.einsum('tij,tjk->tik', residual, item_tiles)
    item_terms = jnp.einsum('tij,tik->tjk', residual, user_tiles)
    pick_user = (tile_user[:, None] == jnp.arange(user_bf.shape[0], dtype=jnp.int32)[None, :]).astype(jnp.float32)
    pick_item = (tile_item[:, None] == jnp.arange(item_bf.shape[0], dtype=jnp.int32)[None, :]).astype(jnp.float32)
    grad_users = jnp.einsum('tn,tik->nik', pick_user, user_terms, precision=lax.Precision.HIGHEST).reshape(-1, width) + DECAY * users
    grad_items = jnp.einsum('tn,tik->nik', pick_item, item_terms, precision=lax.Precision.HIGHEST).reshape(-1, width) + DECAY * items
    user_accum = user_accum + grad_users * grad_users
    item_accum = item_accum + grad_items * grad_items
    users = users - LEARN_RATE * grad_users / jnp.sqrt(user_accum)
    items = items - LEARN_RATE * grad_items / jnp.sqrt(item_accum)
    return (users, user_accum, items, item_accum)

def reference(users, user_accum, items, item_accum, seen_user, seen_item, row_live, col_live, neg_user, neg_item):
    devices = N_BLK * N_XOR
    user_blocks = users.reshape(devices, USER_DEV, K)
    user_sums = user_accum.reshape(devices, USER_DEV, K)
    state = jnp.stack([items, item_accum]).reshape(2, N_BLK, N_XOR, 2, HALF, K)
    seen_u = seen_user.reshape(SUBS, devices, OBS)
    seen_i = seen_item.reshape(SUBS, devices, OBS)
    rows_l = row_live.reshape(SUBS, devices, OBS, TILE)
    cols_l = col_live.reshape(SUBS, devices, OBS, TILE)
    neg_u = neg_user.reshape(SUBS, devices, NEG)
    neg_i = neg_item.reshape(SUBS, devices, NEG)
    for sub_round in range(SUBS):
        flat = state.reshape(2, devices, ITEM_DEV, K)
        result = lax.map(lambda pack: local_step(*pack), (user_blocks, user_sums, flat[0], flat[1], seen_u[sub_round], seen_i[sub_round], rows_l[sub_round], cols_l[sub_round], neg_u[sub_round], neg_i[sub_round]))
        user_blocks, user_sums = (result[0], result[1])
        state = jnp.stack([result[2], result[3]]).reshape(2, N_BLK, N_XOR, 2, HALF, K)
        if sub_round + 1 < SUBS:
            state = jnp.roll(state, 1, axis=1)
            partner = np.arange(N_XOR) ^ 1 << sub_round % 2
            state = state.at[:, :, :, 1].set(state[:, :, partner, 1])
    flat = state.reshape(2, ITEMS, K)
    return (user_blocks.reshape(USERS, K), user_sums.reshape(USERS, K), flat[0], flat[1])
```

```python
import functools

import jax
import jax.numpy as jnp
from jax import lax
from jax.experimental import pallas as pl
from jax.experimental.pallas import tpu as pltpu
from jax.sharding import PartitionSpec as P

SUBS = 6
TILE = 128
HALF = 256
LEARN_RATE = 0.05
DECAY = 0.02
NEG_WEIGHT = 0.25
AXES = ("blk", "xor")
BF = jnp.bfloat16
F32 = jnp.float32


def rows_of(scalars, sub_round, count):
    row = lax.broadcasted_iota(jnp.int32, (count, TILE), 0)
    out = jnp.zeros((count, TILE), jnp.int32)
    for t in range(count):
        out = jnp.where(row == t, scalars[sub_round, t], out)
    return out


def spread(tile, live, first, count):
    return jnp.concatenate([jnp.where(tile == first + n, live, 0.0) for n in range(count)], axis=1)


def pair_factors(sub_round, half, su, si, nu, ni, row_live, col_live, user_tiles):
    obs, neg = su.shape[1], nu.shape[1]
    rows = row_live[sub_round].astype(F32)
    cols = col_live[sub_round].astype(F32)
    ones = jnp.ones((neg, TILE), F32)
    left = jnp.concatenate(
        [
            spread(rows_of(su, sub_round, obs), rows, 0, user_tiles),
            spread(rows_of(nu, sub_round, neg), ones, 0, user_tiles),
        ],
        axis=0,
    ).astype(BF)
    first = half * (HALF // TILE)
    seen = spread(rows_of(si, sub_round, obs), cols, first, HALF // TILE)
    sampled = spread(rows_of(ni, sub_round, neg), ones, first, HALF // TILE)
    right = jnp.concatenate(
        [
            jnp.concatenate([seen, seen], axis=1),
            jnp.concatenate([NEG_WEIGHT * sampled, jnp.zeros_like(sampled)], axis=1),
        ],
        axis=0,
    ).astype(BF)
    return left, right


def adagrad(factor, accum, grad):
    accum = accum + grad * grad
    return factor - LEARN_RATE * grad * lax.rsqrt(accum), accum


def dot(a, b, contract):
    return lax.dot_general(a, b, ((contract[:1], contract[1:]), ((), ())), preferred_element_type=F32)


STEP = 256


def half_kernel(sub_round, half, from_whole, last, *refs):
    refs = list(refs)
    su, si, nu, ni, row_live, col_live, users = refs[:7]
    del refs[:7]
    if from_whole:
        factor_ref, accum_ref = refs[:2]
        del refs[:2]
        factor = factor_ref[half * HALF : (half + 1) * HALF, :]
        accum = accum_ref[half * HALF : (half + 1) * HALF, :]
    else:
        state = refs.pop(0)
        factor = state[:HALF, :]
        accum = state[HALF:, :]
    if half == 1:
        user_accum, grad_in = refs[:2]
        del refs[:2]
        if last:
            other = refs.pop(0)
            users_out, user_accum_out, items_out, item_accum_out = refs
        else:
            users_out, user_accum_out, state_out = refs
    else:
        grad_out, state_out = refs
    left, right = pair_factors(sub_round, half, su, si, nu, ni, row_live, col_live, users.shape[0] // TILE)
    item_bf = factor.astype(BF)
    grad_items = DECAY * factor
    for start in range(0, users.shape[0], STEP):
        at = slice(start, start + STEP)
        user = users[at, :]
        user_bf = user.astype(BF)
        scores = dot(user_bf, item_bf, (1, 1))
        both = dot(left[:, at], right, (0, 0))
        err = (both[:, :HALF] * scores - both[:, HALF:]).astype(BF)
        grad_user = dot(err, item_bf, (1, 0))
        grad_items += dot(err, user_bf, (0, 0))
        if half == 0:
            grad_out[at, :] = grad_user
        else:
            grad = grad_in[at, :] + grad_user + DECAY * user
            users_out[at, :], user_accum_out[at, :] = adagrad(user, user_accum[at, :], grad)
    factor, accum = adagrad(factor, accum, grad_items)
    if half == 1 and last:
        items_out[:HALF, :] = other[:HALF, :]
        item_accum_out[:HALF, :] = other[HALF:, :]
        items_out[HALF:, :] = factor
        item_accum_out[HALF:, :] = accum
    else:
        state_out[:HALF, :] = factor
        state_out[HALF:, :] = accum


def run_half(sub_round, half, idx, users, state, extra=()):
    from_whole = isinstance(state, tuple)
    last = half == 1 and len(extra) == 3
    states = list(state) if from_whole else [state]
    user_shape = jax.ShapeDtypeStruct(users.shape, F32)
    state_shape = jax.ShapeDtypeStruct((2 * HALF, users.shape[1]), F32)
    if half == 0:
        out = [user_shape, state_shape]
    elif last:
        out = [user_shape, user_shape, state_shape, state_shape]
    else:
        out = [user_shape, user_shape, state_shape]
    smem = pl.BlockSpec(memory_space=pltpu.SMEM)
    vmem = pl.BlockSpec(memory_space=pltpu.VMEM)
    operands = [*idx, users, *states, *extra]
    size = users.shape[0] * HALF * users.shape[1]
    return pl.pallas_call(
        functools.partial(half_kernel, sub_round, half, from_whole, last),
        out_shape=out,
        in_specs=[smem] * 4 + [vmem] * (len(operands) - 4),
        out_specs=[vmem] * len(out),
        compiler_params=pltpu.CompilerParams(vmem_limit_bytes=24 * 1024 * 1024),
        cost_estimate=pl.CostEstimate(flops=10 * size, bytes_accessed=6 * 1024 * 1024, transcendentals=0),
        name="half_b" if half else "half_a",
    )(*operands)


def move(state, sub_round, half):
    blks, xors = lax.axis_size("blk"), lax.axis_size("xor")
    flip = 2 ** (sub_round % 2) if half == 1 else 0
    pairs = [
        (b * xors + x, ((b + 1) % blks) * xors + (x ^ flip)) for b in range(blks) for x in range(xors)
    ]
    return lax.ppermute(state, AXES, pairs)


def per_device(
    users,
    user_accum,
    items,
    item_accum,
    seen_user,
    seen_item,
    row_live,
    col_live,
    neg_user,
    neg_item,
):
    idx = (seen_user, seen_item, neg_user, neg_item, row_live, col_live)
    a = b = (items, item_accum)
    for s in range(SUBS):
        grad, a = run_half(s, 0, idx, users, a)
        if s + 1 < SUBS:
            a = move(a, s, 0)
            users, user_accum, b = run_half(s, 1, idx, users, b, (user_accum, grad))
            b = move(b, s, 1)
        else:
            return tuple(run_half(s, 1, idx, users, b, (user_accum, grad, a)))


def solution(mesh):
    rows = P(AXES, None)
    placed = (rows,) * 4 + (P(None, AXES),) * 2 + (P(None, AXES, None),) * 2 + (P(None, AXES),) * 2
    return jax.shard_map(
        per_device, mesh=mesh, in_specs=placed, out_specs=(rows,) * 4, check_vma=False
    )
```

```python
import functools

import jax
import jax.numpy as jnp
from jax import lax
from jax.experimental import pallas as pl
from jax.experimental.pallas import tpu as pltpu
from jax.sharding import PartitionSpec as P

SUBS = 6
TILE = 128
CHUNK = 128
STEP = 256
LEARN_RATE = 0.05
DECAY = 0.02
NEG_WEIGHT = 0.25
AXES = ("blk", "xor")
BF = jnp.bfloat16
F32 = jnp.float32


def rows_of(scalars, sub_round, count):
    row = lax.broadcasted_iota(jnp.int32, (count, TILE), 0)
    out = jnp.zeros((count, TILE), jnp.int32)
    for t in range(count):
        out = jnp.where(row == t, scalars[sub_round, t], out)
    return out


def spread(tile, live, first, count):
    groups = [jnp.where(tile == first + n, live, 0.0) for n in range(count)]
    return groups[0] if count == 1 else jnp.concatenate(groups, axis=1)


def pair_factors(sub_round, chunk, su, si, nu, ni, row_live, col_live, user_tiles):
    obs, neg = su.shape[1], nu.shape[1]
    rows = row_live[sub_round].astype(F32)
    cols = col_live[sub_round].astype(F32)
    ones = jnp.ones((neg, TILE), F32)
    left = jnp.concatenate(
        [
            spread(rows_of(su, sub_round, obs), rows, 0, user_tiles),
            spread(rows_of(nu, sub_round, neg), ones, 0, user_tiles),
        ],
        axis=0,
    ).astype(BF)
    count = CHUNK // TILE
    seen = spread(rows_of(si, sub_round, obs), cols, chunk * count, count)
    sampled = spread(rows_of(ni, sub_round, neg), ones, chunk * count, count)
    right = jnp.concatenate(
        [
            jnp.concatenate([seen, seen], axis=1),
            jnp.concatenate([NEG_WEIGHT * sampled, jnp.zeros_like(sampled)], axis=1),
        ],
        axis=0,
    ).astype(BF)
    return left, right


def adagrad(factor, accum, grad):
    accum = accum + grad * grad
    return factor - LEARN_RATE * grad * lax.rsqrt(accum), accum


def dot(a, b, contract):
    return lax.dot_general(a, b, ((contract[:1], contract[1:]), ((), ())), preferred_element_type=F32)


def chunk_kernel(sub_round, chunk, chunks, *refs):
    refs = list(refs)

    def take(count):
        out = refs[:count]
        del refs[:count]
        return out

    first, final = chunk == 0, chunk == chunks - 1
    end = sub_round == SUBS - 1
    su, si, nu, ni, row_live, col_live, users = take(7)
    if sub_round == 0:
        factor_ref, accum_ref = take(2)
        at = slice(chunk * CHUNK, (chunk + 1) * CHUNK)
        if factor_ref.shape[0] == CHUNK:
            at = slice(None)
        factor, accum = factor_ref[at, :], accum_ref[at, :]
    else:
        (state,) = take(1)
        factor, accum = state[:CHUNK, :], state[CHUNK:, :]
    if not first:
        (grad_in,) = take(1)
    if final:
        (user_accum,) = take(1)
        if end:
            others = take(chunks - 1)
        users_out, user_accum_out = take(2)
    else:
        (grad_out,) = take(1)
    left, right = pair_factors(sub_round, chunk, su, si, nu, ni, row_live, col_live, users.shape[0] // TILE)
    item_bf = factor.astype(BF)
    grad_items = DECAY * factor
    for start in range(0, users.shape[0], STEP):
        at = slice(start, start + STEP)
        user = users[at, :]
        user_bf = user.astype(BF)
        scores = dot(user_bf, item_bf, (1, 1))
        both = dot(left[:, at], right, (0, 0))
        err = (both[:, :CHUNK] * scores - both[:, CHUNK:]).astype(BF)
        grad_user = dot(err, item_bf, (1, 0))
        grad_items += dot(err, user_bf, (0, 0))
        if not first:
            grad_user += grad_in[at, :]
        if final:
            grad_user += DECAY * user
            users_out[at, :], user_accum_out[at, :] = adagrad(user, user_accum[at, :], grad_user)
        else:
            grad_out[at, :] = grad_user
    factor, accum = adagrad(factor, accum, grad_items)
    if final and end:
        items_out, item_accum_out = refs
        for n, other in enumerate(others):
            items_out[n * CHUNK : (n + 1) * CHUNK, :] = other[:CHUNK, :]
            item_accum_out[n * CHUNK : (n + 1) * CHUNK, :] = other[CHUNK:, :]
        items_out[chunk * CHUNK :, :] = factor
        item_accum_out[chunk * CHUNK :, :] = accum
    else:
        (state_out,) = refs
        state_out[:CHUNK, :] = factor
        state_out[CHUNK:, :] = accum


def run_chunk(sub_round, chunk, chunks, idx, users, state, extra):
    width = users.shape[1]
    user_shape = jax.ShapeDtypeStruct(users.shape, F32)
    state_shape = jax.ShapeDtypeStruct((2 * CHUNK, width), F32)
    final, end = chunk == chunks - 1, sub_round == SUBS - 1
    out = [user_shape] * (2 if final else 1)
    if final and end:
        out += [jax.ShapeDtypeStruct((chunks * CHUNK, width), F32)] * 2
    else:
        out += [state_shape]
    smem = pl.BlockSpec(memory_space=pltpu.SMEM)
    vmem = pl.BlockSpec(memory_space=pltpu.VMEM)
    operands = [*idx, users, *state, *extra]
    in_specs = [smem] * 4 + [vmem] * (len(operands) - 4)
    out_specs = [vmem] * len(out)
    grid = ()
    if sub_round == 0 and chunk == 0:
        grid = (1,)
        whole = lambda x: pl.BlockSpec(x.shape, lambda i: (0,) * len(x.shape))
        part = pl.BlockSpec((CHUNK, width), lambda i: (0, 0))
        live = pl.BlockSpec((1, *idx[4].shape[1:]), lambda i: (0, 0, 0))
        in_specs = [smem] * 4 + [live] * 2 + [whole(users), part, part]
        out_specs = [whole(x) for x in out]
    size = users.shape[0] * CHUNK * width
    return pl.pallas_call(
        functools.partial(chunk_kernel, sub_round, chunk, chunks),
        grid=grid,
        out_shape=out,
        in_specs=in_specs,
        out_specs=out_specs,
        compiler_params=pltpu.CompilerParams(vmem_limit_bytes=24 * 1024 * 1024),
        cost_estimate=pl.CostEstimate(flops=10 * size, bytes_accessed=6 * 1024 * 1024, transcendentals=0),
        name=f"sub{sub_round}_chunk{chunk}",
    )(*operands)


def move(state, sub_round, second_half):
    blks, xors = lax.axis_size("blk"), lax.axis_size("xor")
    flip = 2 ** (sub_round % 2) if second_half else 0
    pairs = [
        (b * xors + x, ((b + 1) % blks) * xors + (x ^ flip)) for b in range(blks) for x in range(xors)
    ]
    return lax.ppermute(state, AXES, pairs)


def per_device(
    users,
    user_accum,
    items,
    item_accum,
    seen_user,
    seen_item,
    row_live,
    col_live,
    neg_user,
    neg_item,
):
    idx = (seen_user, seen_item, neg_user, neg_item, row_live, col_live)
    chunks = items.shape[0] // CHUNK
    states = [(items, item_accum)] * chunks
    for s in range(SUBS):
        grad = ()
        moved = []
        for n in range(chunks):
            final, end = n == chunks - 1, s == SUBS - 1
            extra = (*grad, user_accum) if final else grad
            if final and end:
                return tuple(run_chunk(s, n, chunks, idx, users, states[n], (*extra, *(m[0] for m in moved))))
            *grad, state = run_chunk(s, n, chunks, idx, users, states[n], extra)
            if not end:
                state = move(state, s, n >= chunks // 2)
            moved.append((state,))
        users, user_accum = grad
        states = moved


def solution(mesh):
    rows = P(AXES, None)
    placed = (rows,) * 4 + (P(None, AXES),) * 2 + (P(None, AXES, None),) * 2 + (P(None, AXES),) * 2
    return jax.shard_map(
        per_device, mesh=mesh, in_specs=placed, out_specs=(rows,) * 4, check_vma=False
    )
```

```python
import functools

import jax
import jax.numpy as jnp
from jax import lax
from jax.experimental import pallas as pl
from jax.experimental.pallas import tpu as pltpu
from jax.sharding import PartitionSpec as P

SUBS = 6
TILE = 128
CHUNK = 128
STEP = 256
LEARN_RATE = 0.05
DECAY = 0.02
NEG_WEIGHT = 0.25
AXES = ("blk", "xor")
ORDERS = ((0, 2, 1, 3),) * SUBS
BF = jnp.bfloat16
F32 = jnp.float32
VMEM_SPEC = pl.BlockSpec(memory_space=pltpu.VMEM)
HBM_SPEC = pl.BlockSpec(memory_space=pltpu.HBM)
PARAMS = pltpu.CompilerParams(vmem_limit_bytes=24 * 1024 * 1024)


def down(row):
    count = row.shape[1]
    values = jnp.broadcast_to(row.astype(F32), (count, count))
    here = lax.broadcasted_iota(jnp.int32, (count, count), 0) == lax.broadcasted_iota(
        jnp.int32, (count, count), 1
    )
    column = jnp.sum(jnp.where(here, values, 0.0), axis=1, keepdims=True)
    return jnp.broadcast_to(column, (count, TILE))


def spread(tile, live, first, count):
    groups = [jnp.where(tile == first + n, live, 0.0) for n in range(count)]
    return groups[0] if count == 1 else jnp.concatenate(groups, axis=1)


def pair_factors(s, su, si, nu, ni, row_live, col_live, user_tiles, chunks):
    rows = row_live[s].astype(F32)
    cols = col_live[s].astype(F32)
    ones = jnp.ones((nu.shape[1], TILE), F32)
    at = slice(s, s + 1)
    left = jnp.concatenate(
        [
            spread(down(su[at, :]), rows, 0, user_tiles),
            spread(down(nu[at, :]), ones, 0, user_tiles),
        ],
        axis=0,
    )
    count = CHUNK // TILE
    item, sampled_item = down(si[at, :]), down(ni[at, :])
    rights = []
    for chunk in range(chunks):
        seen = spread(item, cols, chunk * count, count)
        sampled = spread(sampled_item, ones, chunk * count, count)
        rights.append(
            jnp.concatenate(
                [
                    jnp.concatenate([seen, seen], axis=1),
                    jnp.concatenate([NEG_WEIGHT * sampled, jnp.zeros_like(sampled)], axis=1),
                ],
                axis=0,
            ).astype(BF)
        )
    return left.T.astype(BF), rights


def adagrad(factor, accum, grad):
    accum = accum + grad * grad
    return factor - LEARN_RATE * grad * lax.rsqrt(accum), accum


def dot(a, b, contract):
    return lax.dot_general(a, b, ((contract[:1], contract[1:]), ((), ())), preferred_element_type=F32)


def chunk_terms(users, left, right, factor, each):
    item_bf = factor.astype(BF)
    grad_items = DECAY * factor
    for start in range(0, users.shape[0], STEP):
        at = slice(start, start + STEP)
        user = users[at, :]
        user_bf = user.astype(BF)
        scores = dot(user_bf, item_bf, (1, 1))
        both = dot(left[at, :], right, (1, 0))
        err = (both[:, :CHUNK] * scores - both[:, CHUNK:]).astype(BF)
        each(at, user, dot(err, item_bf, (1, 0)))
        grad_items += dot(err, user_bf, (0, 0))
    return grad_items


def store_state(state, factor, accum):
    state[:CHUNK, :] = factor
    state[CHUNK:, :] = accum


def first_kernel(chunks, *refs):
    args, outs, scratch = refs[:10], refs[10 : 10 + 5 + chunks], refs[10 + 5 + chunks :]
    users_hbm, user_accum_hbm, items_hbm, item_accum_hbm = args[:4]
    users, user_accum, left_out, right_out, grad_out, *states = outs
    small, (raw, sems) = scratch[:6], scratch[6:]
    copies = [pltpu.make_async_copy(src, dst, sems.at[n]) for n, (src, dst) in enumerate(zip(args[4:], small))]
    copies.append(pltpu.make_async_copy(users_hbm, users, sems.at[6]))
    at = 7
    for chunk in range(chunks):
        target = raw if chunk == 0 else states[chunk]
        rows = pl.ds(chunk * CHUNK, CHUNK)
        for part, source in enumerate((items_hbm, item_accum_hbm)):
            copies.append(
                pltpu.make_async_copy(
                    source.at[rows], target.at[pl.ds(part * CHUNK, CHUNK)], sems.at[at]
                )
            )
            at += 1
    copies.append(pltpu.make_async_copy(user_accum_hbm, user_accum, sems.at[at]))
    for copy in copies:
        copy.start()
    for copy in copies[:6]:
        copy.wait()
    su, si, row_live, col_live, nu, ni = small
    left, rights = pair_factors(0, su, si, nu, ni, row_live, col_live, users.shape[0] // TILE, chunks)
    left_out[...] = left
    for chunk in range(chunks):
        right_out[chunk] = rights[chunk]
    for copy in copies[6:9]:
        copy.wait()
    factor, accum = raw[:CHUNK, :], raw[CHUNK:, :]

    def each(at, user, grad):
        grad_out[at, :] = grad

    grad_items = chunk_terms(users, left_out, rights[0], factor, each)
    store_state(states[0], *adagrad(factor, accum, grad_items))
    for copy in copies[9:]:
        copy.wait()


def run_first(args):
    users, user_accum, items, item_accum, *small = args
    width = users.shape[1]
    chunks = items.shape[0] // CHUNK
    terms = small[0].shape[1] + small[4].shape[1]
    sds = jax.ShapeDtypeStruct
    out = [
        sds(users.shape, F32),
        sds(users.shape, F32),
        sds((users.shape[0], terms), BF),
        sds((chunks, terms, 2 * CHUNK), BF),
        sds(users.shape, F32),
    ] + [sds((2 * CHUNK, width), F32)] * chunks
    return pl.pallas_call(
        functools.partial(first_kernel, chunks),
        out_shape=out,
        in_specs=[HBM_SPEC] * len(args),
        out_specs=[VMEM_SPEC] * len(out),
        scratch_shapes=[pltpu.VMEM(x.shape, x.dtype) for x in small]
        + [pltpu.VMEM((2 * CHUNK, width), F32), pltpu.SemaphoreType.DMA((8 + 2 * chunks,))],
        compiler_params=PARAMS,
        name="first_chunk",
    )(*(pltpu.with_memory_space_constraint(x, pltpu.HBM) for x in args))


def factors_kernel(user_tiles, chunks, *refs):
    args, (left_out, right_out), (*small, sems) = refs[:6], refs[7:9], refs[9:]
    copies = [pltpu.make_async_copy(src, dst, sems.at[n]) for n, (src, dst) in enumerate(zip(args, small))]
    for copy in copies:
        copy.start()
    for copy in copies:
        copy.wait()
    su, si, row_live, col_live, nu, ni = small
    for s in range(1, SUBS):
        left, rights = pair_factors(s, su, si, nu, ni, row_live, col_live, user_tiles, chunks)
        left_out[s - 1] = left
        for chunk in range(chunks):
            right_out[s - 1, chunk] = rights[chunk]


def run_factors(small, user_rows, chunks, after):
    terms = small[0].shape[1] + small[4].shape[1]
    pinned = [pltpu.with_memory_space_constraint(x, pltpu.HBM) for x in small]
    return pl.pallas_call(
        functools.partial(factors_kernel, user_rows // TILE, chunks),
        out_shape=[
            jax.ShapeDtypeStruct((SUBS - 1, user_rows, terms), BF),
            jax.ShapeDtypeStruct((SUBS - 1, chunks, terms, 2 * CHUNK), BF),
        ],
        in_specs=[HBM_SPEC] * 6 + [pl.BlockSpec(memory_space=pl.ANY)],
        out_specs=[VMEM_SPEC] * 2,
        scratch_shapes=[pltpu.VMEM(x.shape, x.dtype) for x in small] + [pltpu.SemaphoreType.DMA((6,))],
        compiler_params=PARAMS,
        name="pair_factors",
    )(*pinned, after)


def chunk_kernel(s, chunk, first, final, chunks, *refs):
    users, left, right, state, *refs = refs
    if s > 0:
        left, right = left.at[s - 1], right.at[s - 1]
    right = right[chunk]
    if not first:
        grad_in, *refs = refs
    if final:
        user_accum, *refs = refs
    end = final and s == SUBS - 1
    if end:
        others, refs = refs[: chunks - 1], refs[chunks - 1 :]
        outs, (users_out, user_accum_out, state_out, sems) = refs[:4], refs[4:]
        copies = []

        def send(src, dst):
            copies.append(pltpu.make_async_copy(src, dst, sems.at[len(copies)]))
            copies[-1].start()

        for n, other in zip([n for n in range(chunks) if n != chunk], others):
            for part in range(2):
                send(other.at[pl.ds(part * CHUNK, CHUNK)], outs[2 + part].at[pl.ds(n * CHUNK, CHUNK)])
    elif final:
        users_out, user_accum_out, state_out = refs
    else:
        grad_out, state_out = refs
    factor, accum = state[:CHUNK, :], state[CHUNK:, :]

    def each(at, user, grad):
        if not first:
            grad += grad_in[at, :]
        if final:
            grad += DECAY * user
            users_out[at, :], user_accum_out[at, :] = adagrad(user, user_accum[at, :], grad)
            if end:
                rows = pl.ds(at.start, STEP)
                send(users_out.at[rows], outs[0].at[rows])
                send(user_accum_out.at[rows], outs[1].at[rows])
        else:
            grad_out[at, :] = grad

    grad_items = chunk_terms(users, left, right, factor, each)
    store_state(state_out, *adagrad(factor, accum, grad_items))
    if end:
        for part in range(2):
            send(state_out.at[pl.ds(part * CHUNK, CHUNK)], outs[2 + part].at[pl.ds(chunk * CHUNK, CHUNK)])
        for copy in copies:
            copy.wait()


def run_chunk(s, chunk, first, final, chunks, users, factors, state, extra):
    width = users.shape[1]
    user_shape = jax.ShapeDtypeStruct(users.shape, F32)
    state_shape = jax.ShapeDtypeStruct((2 * CHUNK, width), F32)
    end = final and s == SUBS - 1
    out = [user_shape] * (2 if final else 1)
    out += [jax.ShapeDtypeStruct((chunks * CHUNK, width), F32)] * 2 if end else [state_shape]
    scratch = []
    if end:
        copies = 2 * chunks + 2 * (users.shape[0] // STEP)
        scratch = [pltpu.VMEM(x.shape, F32) for x in (users, users, state)]
        scratch.append(pltpu.SemaphoreType.DMA((copies,)))
    operands = [users, *factors, state, *extra]
    return pl.pallas_call(
        functools.partial(chunk_kernel, s, chunk, first, final, chunks),
        out_shape=out,
        in_specs=[VMEM_SPEC] * len(operands),
        out_specs=[HBM_SPEC if end else VMEM_SPEC] * len(out),
        scratch_shapes=scratch,
        compiler_params=PARAMS,
        cost_estimate=pl.CostEstimate(
            flops=10 * users.shape[0] * CHUNK * width, bytes_accessed=6 * 1024 * 1024, transcendentals=0
        ),
        name=f"sub{s}_chunk{chunk}",
    )(*operands)


def move(state, s, second_half):
    blks, xors = lax.axis_size("blk"), lax.axis_size("xor")
    flip = 2 ** (s % 2) if second_half else 0
    pairs = [
        (b * xors + x, ((b + 1) % blks) * xors + (x ^ flip)) for b in range(blks) for x in range(xors)
    ]
    return lax.ppermute(state, AXES, pairs)


def per_device(*args):
    chunks = args[2].shape[0] // CHUNK
    users, user_accum, left, right, grad, *states = run_first(args)
    factors = (left, right)
    grad = [grad]
    for s, order in enumerate(ORDERS):
        moved = [None] * chunks
        for n in order:
            first, final = n == order[0], n == order[-1]
            extra = (*grad, user_accum) if final else grad
            end = s == SUBS - 1
            if final and end:
                extra = (*extra, *(m for m in moved if m is not None))
                return tuple(run_chunk(s, n, first, final, chunks, users, factors, states[n], extra))
            state = states[n]
            if s > 0 or not first:
                *grad, state = run_chunk(s, n, first, final, chunks, users, factors, state, extra)
            moved[n] = state if end else move(state, s, n >= chunks // 2)
        users, user_accum = grad
        grad = []
        states = moved
        if s == 0:
            factors = run_factors(args[4:], users.shape[0], chunks, users)


def solution(mesh):
    rows = P(AXES, None)
    placed = (rows,) * 4 + (P(None, AXES),) * 2 + (P(None, AXES, None),) * 2 + (P(None, AXES),) * 2
    return jax.shard_map(
        per_device, mesh=mesh, in_specs=placed, out_specs=(rows,) * 4, check_vma=False
    )
```

```python
import functools

import jax
import jax.numpy as jnp
from jax import lax
from jax.experimental import pallas as pl
from jax.experimental.pallas import tpu as pltpu
from jax.sharding import PartitionSpec as P

SUBS = 6
TILE = 128
CHUNK = 128
STEP = 256
LEARN_RATE = 0.05
DECAY = 0.02
NEG_WEIGHT = 0.25
AXES = ("blk", "xor")
TURNS, ROWS = (0, 2, 1, 3), (0, 1, 2, 3)
ORDERS = (TURNS, TURNS, ROWS, TURNS, ROWS, TURNS)
BF = jnp.bfloat16
F32 = jnp.float32
VMEM_SPEC = pl.BlockSpec(memory_space=pltpu.VMEM)
HBM_SPEC = pl.BlockSpec(memory_space=pltpu.HBM)
PARAMS = pltpu.CompilerParams(vmem_limit_bytes=24 * 1024 * 1024)


def down(row):
    count = row.shape[1]
    values = jnp.broadcast_to(row.astype(F32), (count, count))
    here = lax.broadcasted_iota(jnp.int32, (count, count), 0) == lax.broadcasted_iota(
        jnp.int32, (count, count), 1
    )
    column = jnp.sum(jnp.where(here, values, 0.0), axis=1, keepdims=True)
    return jnp.broadcast_to(column, (count, TILE))


def spread(tile, live, first, count):
    groups = [jnp.where(tile == first + n, live, 0.0) for n in range(count)]
    return groups[0] if count == 1 else jnp.concatenate(groups, axis=1)


def pair_factors(s, su, si, nu, ni, row_live, col_live, user_tiles, chunks):
    rows = row_live[s].astype(F32)
    cols = col_live[s].astype(F32)
    ones = jnp.ones((nu.shape[1], TILE), F32)
    at = slice(s, s + 1)
    left = jnp.concatenate(
        [
            spread(down(su[at, :]), rows, 0, user_tiles),
            spread(down(nu[at, :]), ones, 0, user_tiles),
        ],
        axis=0,
    )
    count = CHUNK // TILE
    item, sampled_item = down(si[at, :]), down(ni[at, :])
    rights = []
    for chunk in range(chunks):
        seen = spread(item, cols, chunk * count, count)
        sampled = spread(sampled_item, ones, chunk * count, count)
        rights.append(
            jnp.concatenate(
                [
                    jnp.concatenate([seen, seen], axis=1),
                    jnp.concatenate([NEG_WEIGHT * sampled, jnp.zeros_like(sampled)], axis=1),
                ],
                axis=0,
            ).astype(BF)
        )
    return left.T.astype(BF), rights


def adagrad(factor, accum, grad):
    accum = accum + grad * grad
    return factor - LEARN_RATE * grad * lax.rsqrt(accum), accum


def dot(a, b, contract):
    return lax.dot_general(a, b, ((contract[:1], contract[1:]), ((), ())), preferred_element_type=F32)


def chunk_terms(users, left, right, factor, each):
    item_bf = factor.astype(BF)
    grad_items = DECAY * factor
    for start in range(0, users.shape[0], STEP):
        at = slice(start, start + STEP)
        user = users[at, :]
        user_bf = user.astype(BF)
        scores = dot(user_bf, item_bf, (1, 1))
        both = dot(left[at, :], right, (1, 0))
        err = (both[:, :CHUNK] * scores - both[:, CHUNK:]).astype(BF)
        each(at, user, dot(err, item_bf, (1, 0)))
        grad_items += dot(err, user_bf, (0, 0))
    return grad_items


def store_state(state, factor, accum):
    state[:CHUNK, :] = factor
    state[CHUNK:, :] = accum


def first_kernel(chunks, *refs):
    args, outs, scratch = refs[:10], refs[10 : 10 + 5 + chunks], refs[10 + 5 + chunks :]
    users_hbm, user_accum_hbm, items_hbm, item_accum_hbm = args[:4]
    users, user_accum, left_out, right_out, grad_out, *states = outs
    small, (raw, sems) = scratch[:6], scratch[6:]
    copies = [pltpu.make_async_copy(src, dst, sems.at[n]) for n, (src, dst) in enumerate(zip(args[4:], small))]
    copies.append(pltpu.make_async_copy(users_hbm, users, sems.at[6]))
    at = 7
    tile = ORDERS[0][0]
    for chunk in (tile, *(n for n in range(chunks) if n != tile)):
        target = raw if chunk == tile else states[chunk]
        rows = pl.ds(chunk * CHUNK, CHUNK)
        for part, source in enumerate((items_hbm, item_accum_hbm)):
            copies.append(
                pltpu.make_async_copy(
                    source.at[rows], target.at[pl.ds(part * CHUNK, CHUNK)], sems.at[at]
                )
            )
            at += 1
    copies.append(pltpu.make_async_copy(user_accum_hbm, user_accum, sems.at[at]))
    for copy in copies:
        copy.start()
    for copy in copies[:6]:
        copy.wait()
    su, si, row_live, col_live, nu, ni = small
    left, rights = pair_factors(0, su, si, nu, ni, row_live, col_live, users.shape[0] // TILE, chunks)
    left_out[...] = left
    for chunk in range(chunks):
        right_out[chunk] = rights[chunk]
    for copy in copies[6:9]:
        copy.wait()
    factor, accum = raw[:CHUNK, :], raw[CHUNK:, :]

    def each(at, user, grad):
        grad_out[at, :] = grad

    grad_items = chunk_terms(users, left_out, rights[tile], factor, each)
    store_state(states[tile], *adagrad(factor, accum, grad_items))
    for copy in copies[9:]:
        copy.wait()


def run_first(args):
    users, user_accum, items, item_accum, *small = args
    width = users.shape[1]
    chunks = items.shape[0] // CHUNK
    terms = small[0].shape[1] + small[4].shape[1]
    sds = jax.ShapeDtypeStruct
    out = [
        sds(users.shape, F32),
        sds(users.shape, F32),
        sds((users.shape[0], terms), BF),
        sds((chunks, terms, 2 * CHUNK), BF),
        sds(users.shape, F32),
    ] + [sds((2 * CHUNK, width), F32)] * chunks
    return pl.pallas_call(
        functools.partial(first_kernel, chunks),
        out_shape=out,
        in_specs=[HBM_SPEC] * len(args),
        out_specs=[VMEM_SPEC] * len(out),
        scratch_shapes=[pltpu.VMEM(x.shape, x.dtype) for x in small]
        + [pltpu.VMEM((2 * CHUNK, width), F32), pltpu.SemaphoreType.DMA((8 + 2 * chunks,))],
        compiler_params=PARAMS,
        name="first_chunk",
    )(*(pltpu.with_memory_space_constraint(x, pltpu.HBM) for x in args))


def factors_kernel(user_tiles, chunks, *refs):
    args, (left_out, right_out), (*small, sems) = refs[:6], refs[7:9], refs[9:]
    copies = [pltpu.make_async_copy(src, dst, sems.at[n]) for n, (src, dst) in enumerate(zip(args, small))]
    for copy in copies:
        copy.start()
    for copy in copies:
        copy.wait()
    su, si, row_live, col_live, nu, ni = small
    for s in range(1, SUBS):
        left, rights = pair_factors(s, su, si, nu, ni, row_live, col_live, user_tiles, chunks)
        left_out[s - 1] = left
        for chunk in range(chunks):
            right_out[s - 1, chunk] = rights[chunk]


def run_factors(small, user_rows, chunks, after):
    terms = small[0].shape[1] + small[4].shape[1]
    pinned = [pltpu.with_memory_space_constraint(x, pltpu.HBM) for x in small]
    return pl.pallas_call(
        functools.partial(factors_kernel, user_rows // TILE, chunks),
        out_shape=[
            jax.ShapeDtypeStruct((SUBS - 1, user_rows, terms), BF),
            jax.ShapeDtypeStruct((SUBS - 1, chunks, terms, 2 * CHUNK), BF),
        ],
        in_specs=[HBM_SPEC] * 6 + [pl.BlockSpec(memory_space=pl.ANY)],
        out_specs=[VMEM_SPEC] * 2,
        scratch_shapes=[pltpu.VMEM(x.shape, x.dtype) for x in small] + [pltpu.SemaphoreType.DMA((6,))],
        compiler_params=PARAMS,
        name="pair_factors",
    )(*pinned, after)


def chunk_kernel(s, chunk, first, final, chunks, *refs):
    users, left, right, state, *refs = refs
    if s > 0:
        left, right = left.at[s - 1], right.at[s - 1]
    right = right[chunk]
    if not first:
        grad_in, *refs = refs
    if final:
        user_accum, *refs = refs
    end = final and s == SUBS - 1
    if end:
        others, refs = refs[: chunks - 1], refs[chunks - 1 :]
        outs, (users_out, user_accum_out, state_out, sems) = refs[:4], refs[4:]
        copies = []

        def send(src, dst):
            copies.append(pltpu.make_async_copy(src, dst, sems.at[len(copies)]))
            copies[-1].start()

        for n, other in zip([n for n in range(chunks) if n != chunk], others):
            for part in range(2):
                send(other.at[pl.ds(part * CHUNK, CHUNK)], outs[2 + part].at[pl.ds(n * CHUNK, CHUNK)])
    elif final:
        users_out, user_accum_out, state_out = refs
    else:
        grad_out, state_out = refs
    factor, accum = state[:CHUNK, :], state[CHUNK:, :]

    def each(at, user, grad):
        if not first:
            grad += grad_in[at, :]
        if final:
            grad += DECAY * user
            users_out[at, :], user_accum_out[at, :] = adagrad(user, user_accum[at, :], grad)
            if end:
                rows = pl.ds(at.start, STEP)
                send(users_out.at[rows], outs[0].at[rows])
                send(user_accum_out.at[rows], outs[1].at[rows])
        else:
            grad_out[at, :] = grad

    grad_items = chunk_terms(users, left, right, factor, each)
    store_state(state_out, *adagrad(factor, accum, grad_items))
    if end:
        for part in range(2):
            send(state_out.at[pl.ds(part * CHUNK, CHUNK)], outs[2 + part].at[pl.ds(chunk * CHUNK, CHUNK)])
        for copy in copies:
            copy.wait()


def run_chunk(s, chunk, first, final, chunks, users, factors, state, extra):
    width = users.shape[1]
    user_shape = jax.ShapeDtypeStruct(users.shape, F32)
    state_shape = jax.ShapeDtypeStruct((2 * CHUNK, width), F32)
    end = final and s == SUBS - 1
    out = [user_shape] * (2 if final else 1)
    out += [jax.ShapeDtypeStruct((chunks * CHUNK, width), F32)] * 2 if end else [state_shape]
    scratch = []
    if end:
        copies = 2 * chunks + 2 * (users.shape[0] // STEP)
        scratch = [pltpu.VMEM(x.shape, F32) for x in (users, users, state)]
        scratch.append(pltpu.SemaphoreType.DMA((copies,)))
    operands = [users, *factors, state, *extra]
    return pl.pallas_call(
        functools.partial(chunk_kernel, s, chunk, first, final, chunks),
        out_shape=out,
        in_specs=[VMEM_SPEC] * len(operands),
        out_specs=[HBM_SPEC if end else VMEM_SPEC] * len(out),
        scratch_shapes=scratch,
        compiler_params=PARAMS,
        cost_estimate=pl.CostEstimate(
            flops=10 * users.shape[0] * CHUNK * width, bytes_accessed=6 * 1024 * 1024, transcendentals=0
        ),
        name=f"sub{s}_chunk{chunk}",
    )(*operands)


def move(state, s, second_half):
    blks, xors = lax.axis_size("blk"), lax.axis_size("xor")
    flip = 2 ** (s % 2) if second_half else 0
    pairs = [
        (b * xors + x, ((b + 1) % blks) * xors + (x ^ flip)) for b in range(blks) for x in range(xors)
    ]
    return lax.ppermute(state, AXES, pairs)


def per_device(*args):
    chunks = args[2].shape[0] // CHUNK
    users, user_accum, left, right, grad, *states = run_first(args)
    factors = (left, right)
    grad = [grad]
    for s, order in enumerate(ORDERS):
        moved = [None] * chunks
        for n in order:
            first, final = n == order[0], n == order[-1]
            extra = (*grad, user_accum) if final else grad
            end = s == SUBS - 1
            if final and end:
                extra = (*extra, *(m for m in moved if m is not None))
                return tuple(run_chunk(s, n, first, final, chunks, users, factors, states[n], extra))
            state = states[n]
            if s > 0 or not first:
                *grad, state = run_chunk(s, n, first, final, chunks, users, factors, state, extra)
            moved[n] = state if end else move(state, s, n >= chunks // 2)
        users, user_accum = grad
        grad = []
        states = moved
        if s == 0:
            factors = run_factors(args[4:], users.shape[0], chunks, users)


def solution(mesh):
    rows = P(AXES, None)
    placed = (rows,) * 4 + (P(None, AXES),) * 2 + (P(None, AXES, None),) * 2 + (P(None, AXES),) * 2
    return jax.shard_map(
        per_device, mesh=mesh, in_specs=placed, out_specs=(rows,) * 4, check_vma=False
    )
```

```python
import functools

import jax
import jax.numpy as jnp
from jax import lax
from jax.experimental import pallas as pl
from jax.experimental.pallas import tpu as pltpu
from jax.sharding import PartitionSpec as P

SUBS = 6
TILE = 128
CHUNK = 128
STEP = 256
LEARN_RATE = 0.05
DECAY = 0.02
NEG_WEIGHT = 0.25
AXES = ("blk", "xor")
TURNS, ROWS = (0, 2, 1, 3), (0, 1, 2, 3)
ORDERS = (TURNS, TURNS, ROWS, TURNS, ROWS, TURNS)
BF = jnp.bfloat16
F32 = jnp.float32
VMEM_SPEC = pl.BlockSpec(memory_space=pltpu.VMEM)
HBM_SPEC = pl.BlockSpec(memory_space=pltpu.HBM)
PARAMS = pltpu.CompilerParams(vmem_limit_bytes=24 * 1024 * 1024)


def down(row):
    count = row.shape[1]
    values = jnp.broadcast_to(row.astype(F32), (count, count))
    here = lax.broadcasted_iota(jnp.int32, (count, count), 0) == lax.broadcasted_iota(
        jnp.int32, (count, count), 1
    )
    column = jnp.sum(jnp.where(here, values, 0.0), axis=1, keepdims=True)
    return jnp.broadcast_to(column, (count, TILE))


def spread(tile, live, first, count):
    groups = [jnp.where(tile == first + n, live, 0.0) for n in range(count)]
    return groups[0] if count == 1 else jnp.concatenate(groups, axis=1)


def padded(terms):
    return -(-terms // 16) * 16


def pair_factors(s, su, si, nu, ni, row_live, col_live, user_tiles, chunks):
    rows = row_live[s].astype(F32)
    cols = col_live[s].astype(F32)
    ones = jnp.ones((nu.shape[1], TILE), F32)
    at = slice(s, s + 1)
    spare = padded(su.shape[1] + nu.shape[1]) - su.shape[1] - nu.shape[1]
    left = jnp.concatenate(
        [
            spread(down(su[at, :]), rows, 0, user_tiles),
            spread(down(nu[at, :]), ones, 0, user_tiles),
            jnp.zeros((spare, user_tiles * TILE), F32),
        ],
        axis=0,
    )
    count = CHUNK // TILE
    item, sampled_item = down(si[at, :]), down(ni[at, :])
    rights = []
    for chunk in range(chunks):
        seen = spread(item, cols, chunk * count, count)
        sampled = spread(sampled_item, ones, chunk * count, count)
        rights.append(
            jnp.concatenate(
                [
                    jnp.concatenate([seen, seen], axis=1),
                    jnp.concatenate([NEG_WEIGHT * sampled, jnp.zeros_like(sampled)], axis=1),
                    jnp.zeros((spare, 2 * CHUNK), F32),
                ],
                axis=0,
            ).astype(BF)
        )
    return left.T.astype(BF), rights


def adagrad(factor, accum, grad):
    accum = accum + grad * grad
    return factor - LEARN_RATE * grad * lax.rsqrt(accum), accum


def dot(a, b, contract):
    return lax.dot_general(a, b, ((contract[:1], contract[1:]), ((), ())), preferred_element_type=F32)


def chunk_terms(users, left, right, factor, each):
    item_bf = factor.astype(BF)
    grad_items = DECAY * factor
    for start in range(0, users.shape[0], STEP):
        at = slice(start, start + STEP)
        user = users[at, :]
        user_bf = user.astype(BF)
        scores = dot(user_bf, item_bf, (1, 1))
        both = dot(left[at, :], right, (1, 0))
        err = (both[:, :CHUNK] * scores - both[:, CHUNK:]).astype(BF)
        each(at, user, dot(err, item_bf, (1, 0)))
        grad_items += dot(err, user_bf, (0, 0))
    return grad_items


def store_state(state, factor, accum):
    state[:CHUNK, :] = factor
    state[CHUNK:, :] = accum


def first_kernel(chunks, *refs):
    args, outs, scratch = refs[:10], refs[10 : 10 + 5 + chunks], refs[10 + 5 + chunks :]
    users_hbm, user_accum_hbm, items_hbm, item_accum_hbm = args[:4]
    users, user_accum, left_out, right_out, grad_out, *states = outs
    small, (raw, sems) = scratch[:6], scratch[6:]
    copies = [pltpu.make_async_copy(src, dst, sems.at[n]) for n, (src, dst) in enumerate(zip(args[4:], small))]
    copies.append(pltpu.make_async_copy(users_hbm, users, sems.at[6]))
    at = 7
    tile = ORDERS[0][0]
    for chunk in (tile, *(n for n in range(chunks) if n != tile)):
        target = raw if chunk == tile else states[chunk]
        rows = pl.ds(chunk * CHUNK, CHUNK)
        for part, source in enumerate((items_hbm, item_accum_hbm)):
            copies.append(
                pltpu.make_async_copy(
                    source.at[rows], target.at[pl.ds(part * CHUNK, CHUNK)], sems.at[at]
                )
            )
            at += 1
    copies.append(pltpu.make_async_copy(user_accum_hbm, user_accum, sems.at[at]))
    for copy in copies:
        copy.start()
    for copy in copies[:6]:
        copy.wait()
    su, si, row_live, col_live, nu, ni = small
    left, rights = pair_factors(0, su, si, nu, ni, row_live, col_live, users.shape[0] // TILE, chunks)
    left_out[...] = left
    for chunk in range(chunks):
        right_out[chunk] = rights[chunk]
    for copy in copies[6:9]:
        copy.wait()
    factor, accum = raw[:CHUNK, :], raw[CHUNK:, :]

    def each(at, user, grad):
        grad_out[at, :] = grad

    grad_items = chunk_terms(users, left_out, rights[tile], factor, each)
    store_state(states[tile], *adagrad(factor, accum, grad_items))
    for copy in copies[9:]:
        copy.wait()


def run_first(args):
    users, user_accum, items, item_accum, *small = args
    width = users.shape[1]
    chunks = items.shape[0] // CHUNK
    terms = padded(small[0].shape[1] + small[4].shape[1])
    sds = jax.ShapeDtypeStruct
    out = [
        sds(users.shape, F32),
        sds(users.shape, F32),
        sds((users.shape[0], terms), BF),
        sds((chunks, terms, 2 * CHUNK), BF),
        sds(users.shape, F32),
    ] + [sds((2 * CHUNK, width), F32)] * chunks
    return pl.pallas_call(
        functools.partial(first_kernel, chunks),
        out_shape=out,
        in_specs=[HBM_SPEC] * len(args),
        out_specs=[VMEM_SPEC] * len(out),
        scratch_shapes=[pltpu.VMEM(x.shape, x.dtype) for x in small]
        + [pltpu.VMEM((2 * CHUNK, width), F32), pltpu.SemaphoreType.DMA((8 + 2 * chunks,))],
        compiler_params=PARAMS,
        name="first_chunk",
    )(*(pltpu.with_memory_space_constraint(x, pltpu.HBM) for x in args))


def factors_kernel(user_tiles, chunks, *refs):
    args, (left_out, right_out), (*small, sems) = refs[:6], refs[7:9], refs[9:]
    copies = [pltpu.make_async_copy(src, dst, sems.at[n]) for n, (src, dst) in enumerate(zip(args, small))]
    for copy in copies:
        copy.start()
    for copy in copies:
        copy.wait()
    su, si, row_live, col_live, nu, ni = small
    for s in range(1, SUBS):
        left, rights = pair_factors(s, su, si, nu, ni, row_live, col_live, user_tiles, chunks)
        left_out[s - 1] = left
        for chunk in range(chunks):
            right_out[s - 1, chunk] = rights[chunk]


def run_factors(small, user_rows, chunks, after):
    terms = padded(small[0].shape[1] + small[4].shape[1])
    pinned = [pltpu.with_memory_space_constraint(x, pltpu.HBM) for x in small]
    return pl.pallas_call(
        functools.partial(factors_kernel, user_rows // TILE, chunks),
        out_shape=[
            jax.ShapeDtypeStruct((SUBS - 1, user_rows, terms), BF),
            jax.ShapeDtypeStruct((SUBS - 1, chunks, terms, 2 * CHUNK), BF),
        ],
        in_specs=[HBM_SPEC] * 6 + [pl.BlockSpec(memory_space=pl.ANY)],
        out_specs=[VMEM_SPEC] * 2,
        scratch_shapes=[pltpu.VMEM(x.shape, x.dtype) for x in small] + [pltpu.SemaphoreType.DMA((6,))],
        compiler_params=PARAMS,
        name="pair_factors",
    )(*pinned, after)


def chunk_kernel(s, chunk, first, final, chunks, *refs):
    users, left, right, state, *refs = refs
    if s > 0:
        left, right = left.at[s - 1], right.at[s - 1]
    right = right[chunk]
    if not first:
        grad_in, *refs = refs
    if final:
        user_accum, *refs = refs
    end = final and s == SUBS - 1
    if end:
        others, refs = refs[: chunks - 1], refs[chunks - 1 :]
        outs, (users_out, user_accum_out, state_out, sems) = refs[:4], refs[4:]
        copies = []

        def send(src, dst):
            copies.append(pltpu.make_async_copy(src, dst, sems.at[len(copies)]))
            copies[-1].start()

        for n, other in zip([n for n in range(chunks) if n != chunk], others):
            for part in range(2):
                send(other.at[pl.ds(part * CHUNK, CHUNK)], outs[2 + part].at[pl.ds(n * CHUNK, CHUNK)])
    elif final:
        users_out, user_accum_out, state_out = refs
    else:
        grad_out, state_out = refs
    factor, accum = state[:CHUNK, :], state[CHUNK:, :]

    def each(at, user, grad):
        if not first:
            grad += grad_in[at, :]
        if final:
            grad += DECAY * user
            users_out[at, :], user_accum_out[at, :] = adagrad(user, user_accum[at, :], grad)
            if end:
                rows = pl.ds(at.start, STEP)
                send(users_out.at[rows], outs[0].at[rows])
                send(user_accum_out.at[rows], outs[1].at[rows])
        else:
            grad_out[at, :] = grad

    grad_items = chunk_terms(users, left, right, factor, each)
    store_state(state_out, *adagrad(factor, accum, grad_items))
    if end:
        for part in range(2):
            send(state_out.at[pl.ds(part * CHUNK, CHUNK)], outs[2 + part].at[pl.ds(chunk * CHUNK, CHUNK)])
        for copy in copies:
            copy.wait()


def run_chunk(s, chunk, first, final, chunks, users, factors, state, extra):
    width = users.shape[1]
    user_shape = jax.ShapeDtypeStruct(users.shape, F32)
    state_shape = jax.ShapeDtypeStruct((2 * CHUNK, width), F32)
    end = final and s == SUBS - 1
    out = [user_shape] * (2 if final else 1)
    out += [jax.ShapeDtypeStruct((chunks * CHUNK, width), F32)] * 2 if end else [state_shape]
    scratch = []
    if end:
        copies = 2 * chunks + 2 * (users.shape[0] // STEP)
        scratch = [pltpu.VMEM(x.shape, F32) for x in (users, users, state)]
        scratch.append(pltpu.SemaphoreType.DMA((copies,)))
    operands = [users, *factors, state, *extra]
    return pl.pallas_call(
        functools.partial(chunk_kernel, s, chunk, first, final, chunks),
        out_shape=out,
        in_specs=[VMEM_SPEC] * len(operands),
        out_specs=[HBM_SPEC if end else VMEM_SPEC] * len(out),
        scratch_shapes=scratch,
        compiler_params=PARAMS,
        cost_estimate=pl.CostEstimate(
            flops=10 * users.shape[0] * CHUNK * width, bytes_accessed=6 * 1024 * 1024, transcendentals=0
        ),
        name=f"sub{s}_chunk{chunk}",
    )(*operands)


def move(state, s, second_half):
    blks, xors = lax.axis_size("blk"), lax.axis_size("xor")
    flip = 2 ** (s % 2) if second_half else 0
    pairs = [
        (b * xors + x, ((b + 1) % blks) * xors + (x ^ flip)) for b in range(blks) for x in range(xors)
    ]
    return lax.ppermute(state, AXES, pairs)


def per_device(*args):
    chunks = args[2].shape[0] // CHUNK
    users, user_accum, left, right, grad, *states = run_first(args)
    factors = (left, right)
    grad = [grad]
    for s, order in enumerate(ORDERS):
        moved = [None] * chunks
        for n in order:
            first, final = n == order[0], n == order[-1]
            extra = (*grad, user_accum) if final else grad
            end = s == SUBS - 1
            if final and end:
                extra = (*extra, *(m for m in moved if m is not None))
                return tuple(run_chunk(s, n, first, final, chunks, users, factors, states[n], extra))
            state = states[n]
            if s > 0 or not first:
                *grad, state = run_chunk(s, n, first, final, chunks, users, factors, state, extra)
            moved[n] = state if end else move(state, s, n >= chunks // 2)
        users, user_accum = grad
        grad = []
        states = moved
        if s == 0:
            factors = run_factors(args[4:], users.shape[0], chunks, users)


def solution(mesh):
    rows = P(AXES, None)
    placed = (rows,) * 4 + (P(None, AXES),) * 2 + (P(None, AXES, None),) * 2 + (P(None, AXES),) * 2
    return jax.shard_map(
        per_device, mesh=mesh, in_specs=placed, out_specs=(rows,) * 4, check_vma=False
    )
```

```python
import functools

import jax
import jax.numpy as jnp
from jax import lax
from jax.experimental import pallas as pl
from jax.experimental.pallas import tpu as pltpu
from jax.sharding import PartitionSpec as P

SUBS = 6
TILE = 128
CHUNK = 128
STEP = 256
LEARN_RATE = 0.05
DECAY = 0.02
NEG_WEIGHT = 0.25
AXES = ("blk", "xor")
TURNS, ROWS = (0, 2, 1, 3), (0, 1, 2, 3)
ORDERS = (TURNS, TURNS, ROWS, TURNS, ROWS, TURNS)
BF = jnp.bfloat16
F32 = jnp.float32
VMEM_SPEC = pl.BlockSpec(memory_space=pltpu.VMEM)
HBM_SPEC = pl.BlockSpec(memory_space=pltpu.HBM)
PARAMS = pltpu.CompilerParams(vmem_limit_bytes=24 * 1024 * 1024)


def down(row):
    count = row.shape[1]
    values = jnp.broadcast_to(row.astype(F32), (count, count))
    here = lax.broadcasted_iota(jnp.int32, (count, count), 0) == lax.broadcasted_iota(
        jnp.int32, (count, count), 1
    )
    column = jnp.sum(jnp.where(here, values, 0.0), axis=1, keepdims=True)
    return jnp.broadcast_to(column, (count, TILE))


def spread(tile, live, first, count):
    groups = [jnp.where(tile == first + n, live, 0.0) for n in range(count)]
    return groups[0] if count == 1 else jnp.concatenate(groups, axis=1)


def padded(terms):
    return -(-terms // 16) * 16


def pair_factors(s, su, si, nu, ni, row_live, col_live, user_tiles, chunks):
    rows = row_live[s].astype(F32)
    cols = col_live[s].astype(F32)
    ones = jnp.ones((nu.shape[1], TILE), F32)
    at = slice(s, s + 1)
    spare = padded(su.shape[1] + nu.shape[1]) - su.shape[1] - nu.shape[1]
    left = jnp.concatenate(
        [
            spread(down(su[at, :]), rows, 0, user_tiles),
            spread(down(nu[at, :]), ones, 0, user_tiles),
            jnp.zeros((spare, user_tiles * TILE), F32),
        ],
        axis=0,
    )
    count = CHUNK // TILE
    item, sampled_item = down(si[at, :]), down(ni[at, :])
    rights = []
    for chunk in range(chunks):
        seen = spread(item, cols, chunk * count, count)
        sampled = spread(sampled_item, ones, chunk * count, count)
        rights.append(
            jnp.concatenate(
                [
                    jnp.concatenate([seen, seen], axis=1),
                    jnp.concatenate([NEG_WEIGHT * sampled, jnp.zeros_like(sampled)], axis=1),
                    jnp.zeros((spare, 2 * CHUNK), F32),
                ],
                axis=0,
            ).astype(BF)
        )
    return left.T.astype(BF), rights


def adagrad(factor, accum, grad):
    accum = accum + grad * grad
    return factor - LEARN_RATE * grad * lax.rsqrt(accum), accum


def dot(a, b, contract):
    return lax.dot_general(a, b, ((contract[:1], contract[1:]), ((), ())), preferred_element_type=F32)


def chunk_terms(users, left, right, factor, each):
    item_bf = factor.astype(BF)
    grad_items = DECAY * factor
    for start in range(0, users.shape[0], STEP):
        at = slice(start, start + STEP)
        user = users[at, :]
        user_bf = user.astype(BF)
        scores = dot(user_bf, item_bf, (1, 1))
        both = dot(left[at, :], right, (1, 0))
        err = (both[:, :CHUNK] * scores - both[:, CHUNK:]).astype(BF)
        each(at, user, dot(err, item_bf, (1, 0)))
        grad_items += dot(err, user_bf, (0, 0))
    return grad_items


def store_state(state, factor, accum):
    state[:CHUNK, :] = factor
    state[CHUNK:, :] = accum


def first_kernel(chunks, *refs):
    args, outs, scratch = refs[:10], refs[10 : 10 + 5 + chunks], refs[10 + 5 + chunks :]
    users_hbm, user_accum_hbm, items_hbm, item_accum_hbm = args[:4]
    users, user_accum, left_out, right_out, grad_out, *states = outs
    small, (raw, sems) = scratch[:6], scratch[6:]
    copies = []
    for n, (src, dst) in enumerate(zip(args[4:], small)):
        if len(src.shape) == 3:
            src, dst = src.at[pl.ds(0, 1)], dst.at[pl.ds(0, 1)]
        copies.append(pltpu.make_async_copy(src, dst, sems.at[n]))
    copies.append(pltpu.make_async_copy(users_hbm, users, sems.at[6]))
    at = 7
    tile = ORDERS[0][0]
    for chunk in (tile, *(n for n in range(chunks) if n != tile)):
        target = raw if chunk == tile else states[chunk]
        rows = pl.ds(chunk * CHUNK, CHUNK)
        for part, source in enumerate((items_hbm, item_accum_hbm)):
            copies.append(
                pltpu.make_async_copy(
                    source.at[rows], target.at[pl.ds(part * CHUNK, CHUNK)], sems.at[at]
                )
            )
            at += 1
    copies.append(pltpu.make_async_copy(user_accum_hbm, user_accum, sems.at[at]))
    for copy in copies:
        copy.start()
    for copy in copies[:6]:
        copy.wait()
    su, si, row_live, col_live, nu, ni = small
    left, rights = pair_factors(0, su, si, nu, ni, row_live, col_live, users.shape[0] // TILE, chunks)
    left_out[...] = left
    for chunk in range(chunks):
        right_out[chunk] = rights[chunk]
    for copy in copies[6:9]:
        copy.wait()
    factor, accum = raw[:CHUNK, :], raw[CHUNK:, :]

    def each(at, user, grad):
        grad_out[at, :] = grad

    grad_items = chunk_terms(users, left_out, rights[tile], factor, each)
    store_state(states[tile], *adagrad(factor, accum, grad_items))
    for copy in copies[9:]:
        copy.wait()


def run_first(args):
    users, user_accum, items, item_accum, *small = args
    width = users.shape[1]
    chunks = items.shape[0] // CHUNK
    terms = padded(small[0].shape[1] + small[4].shape[1])
    sds = jax.ShapeDtypeStruct
    out = [
        sds(users.shape, F32),
        sds(users.shape, F32),
        sds((users.shape[0], terms), BF),
        sds((chunks, terms, 2 * CHUNK), BF),
        sds(users.shape, F32),
    ] + [sds((2 * CHUNK, width), F32)] * chunks
    return pl.pallas_call(
        functools.partial(first_kernel, chunks),
        out_shape=out,
        in_specs=[HBM_SPEC] * len(args),
        out_specs=[VMEM_SPEC] * len(out),
        scratch_shapes=[pltpu.VMEM(x.shape, x.dtype) for x in small]
        + [pltpu.VMEM((2 * CHUNK, width), F32), pltpu.SemaphoreType.DMA((8 + 2 * chunks,))],
        compiler_params=PARAMS,
        name="first_chunk",
    )(*(pltpu.with_memory_space_constraint(x, pltpu.HBM) for x in args))


def factors_kernel(user_tiles, chunks, *refs):
    args, (left_out, right_out), (*small, sems) = refs[:6], refs[7:9], refs[9:]
    copies = [pltpu.make_async_copy(src, dst, sems.at[n]) for n, (src, dst) in enumerate(zip(args, small))]
    for copy in copies:
        copy.start()
    for copy in copies:
        copy.wait()
    su, si, row_live, col_live, nu, ni = small
    for s in range(1, SUBS):
        left, rights = pair_factors(s, su, si, nu, ni, row_live, col_live, user_tiles, chunks)
        left_out[s - 1] = left
        for chunk in range(chunks):
            right_out[s - 1, chunk] = rights[chunk]


def run_factors(small, user_rows, chunks, after):
    terms = padded(small[0].shape[1] + small[4].shape[1])
    pinned = [pltpu.with_memory_space_constraint(x, pltpu.HBM) for x in small]
    return pl.pallas_call(
        functools.partial(factors_kernel, user_rows // TILE, chunks),
        out_shape=[
            jax.ShapeDtypeStruct((SUBS - 1, user_rows, terms), BF),
            jax.ShapeDtypeStruct((SUBS - 1, chunks, terms, 2 * CHUNK), BF),
        ],
        in_specs=[HBM_SPEC] * 6 + [pl.BlockSpec(memory_space=pl.ANY)],
        out_specs=[VMEM_SPEC] * 2,
        scratch_shapes=[pltpu.VMEM(x.shape, x.dtype) for x in small] + [pltpu.SemaphoreType.DMA((6,))],
        compiler_params=PARAMS,
        name="pair_factors",
    )(*pinned, after)


def chunk_kernel(s, chunk, first, final, chunks, *refs):
    users, left, right, state, *refs = refs
    if s > 0:
        left, right = left.at[s - 1], right.at[s - 1]
    right = right[chunk]
    if not first:
        grad_in, *refs = refs
    if final:
        user_accum, *refs = refs
    end = final and s == SUBS - 1
    if end:
        others, refs = refs[: chunks - 1], refs[chunks - 1 :]
        outs, (users_out, user_accum_out, state_out, sems) = refs[:4], refs[4:]
        copies = []

        def send(src, dst):
            copies.append(pltpu.make_async_copy(src, dst, sems.at[len(copies)]))
            copies[-1].start()

        def send_others():
            for n, other in zip([n for n in range(chunks) if n != chunk], others):
                for part in range(2):
                    send(other.at[pl.ds(part * CHUNK, CHUNK)], outs[2 + part].at[pl.ds(n * CHUNK, CHUNK)])

    elif final:
        users_out, user_accum_out, state_out = refs
    else:
        grad_out, state_out = refs
    factor, accum = state[:CHUNK, :], state[CHUNK:, :]

    def each(at, user, grad):
        if not first:
            grad += grad_in[at, :]
        if final:
            grad += DECAY * user
            users_out[at, :], user_accum_out[at, :] = adagrad(user, user_accum[at, :], grad)
            if end:
                rows = pl.ds(at.start, STEP)
                send(users_out.at[rows], outs[0].at[rows])
                send(user_accum_out.at[rows], outs[1].at[rows])
                if at.start == 0:
                    send_others()
        else:
            grad_out[at, :] = grad

    grad_items = chunk_terms(users, left, right, factor, each)
    store_state(state_out, *adagrad(factor, accum, grad_items))
    if end:
        for part in range(2):
            send(state_out.at[pl.ds(part * CHUNK, CHUNK)], outs[2 + part].at[pl.ds(chunk * CHUNK, CHUNK)])
        for copy in copies:
            copy.wait()


def run_chunk(s, chunk, first, final, chunks, users, factors, state, extra):
    width = users.shape[1]
    user_shape = jax.ShapeDtypeStruct(users.shape, F32)
    state_shape = jax.ShapeDtypeStruct((2 * CHUNK, width), F32)
    end = final and s == SUBS - 1
    out = [user_shape] * (2 if final else 1)
    out += [jax.ShapeDtypeStruct((chunks * CHUNK, width), F32)] * 2 if end else [state_shape]
    scratch = []
    if end:
        copies = 2 * chunks + 2 * (users.shape[0] // STEP)
        scratch = [pltpu.VMEM(x.shape, F32) for x in (users, users, state)]
        scratch.append(pltpu.SemaphoreType.DMA((copies,)))
    operands = [users, *factors, state, *extra]
    return pl.pallas_call(
        functools.partial(chunk_kernel, s, chunk, first, final, chunks),
        out_shape=out,
        in_specs=[VMEM_SPEC] * len(operands),
        out_specs=[HBM_SPEC if end else VMEM_SPEC] * len(out),
        scratch_shapes=scratch,
        compiler_params=PARAMS,
        cost_estimate=pl.CostEstimate(
            flops=10 * users.shape[0] * CHUNK * width, bytes_accessed=6 * 1024 * 1024, transcendentals=0
        ),
        name=f"sub{s}_chunk{chunk}",
    )(*operands)


def move(state, s, second_half):
    blks, xors = lax.axis_size("blk"), lax.axis_size("xor")
    flip = 2 ** (s % 2) if second_half else 0
    pairs = [
        (b * xors + x, ((b + 1) % blks) * xors + (x ^ flip)) for b in range(blks) for x in range(xors)
    ]
    return lax.ppermute(state, AXES, pairs)


def per_device(*args):
    chunks = args[2].shape[0] // CHUNK
    users, user_accum, left, right, grad, *states = run_first(args)
    factors = (left, right)
    grad = [grad]
    for s, order in enumerate(ORDERS):
        moved = [None] * chunks
        for n in order:
            first, final = n == order[0], n == order[-1]
            extra = (*grad, user_accum) if final else grad
            end = s == SUBS - 1
            if final and end:
                extra = (*extra, *(m for m in moved if m is not None))
                return tuple(run_chunk(s, n, first, final, chunks, users, factors, states[n], extra))
            state = states[n]
            if s > 0 or not first:
                *grad, state = run_chunk(s, n, first, final, chunks, users, factors, state, extra)
            moved[n] = state if end else move(state, s, n >= chunks // 2)
        users, user_accum = grad
        grad = []
        states = moved
        if s == 0:
            factors = run_factors(args[4:], users.shape[0], chunks, users)


def solution(mesh):
    rows = P(AXES, None)
    placed = (rows,) * 4 + (P(None, AXES),) * 2 + (P(None, AXES, None),) * 2 + (P(None, AXES),) * 2
    return jax.shard_map(
        per_device, mesh=mesh, in_specs=placed, out_specs=(rows,) * 4, check_vma=False
    )
```

```python
import functools

import jax
import jax.numpy as jnp
from jax import lax
from jax.experimental import pallas as pl
from jax.experimental.pallas import tpu as pltpu
from jax.sharding import PartitionSpec as P

SUBS = 6
TILE = 128
CHUNK = 128
STEP = 256
LEARN_RATE = 0.05
DECAY = 0.02
NEG_WEIGHT = 0.25
AXES = ("blk", "xor")
TURNS, ROWS = (0, 2, 1, 3), (0, 1, 2, 3)
ORDERS = (TURNS, TURNS, ROWS, TURNS, ROWS, TURNS)
BF = jnp.bfloat16
F32 = jnp.float32
VMEM_SPEC = pl.BlockSpec(memory_space=pltpu.VMEM)
HBM_SPEC = pl.BlockSpec(memory_space=pltpu.HBM)
PARAMS = pltpu.CompilerParams(vmem_limit_bytes=24 * 1024 * 1024)


def down(row):
    count = row.shape[1]
    values = jnp.broadcast_to(row.astype(F32), (count, count))
    here = lax.broadcasted_iota(jnp.int32, (count, count), 0) == lax.broadcasted_iota(
        jnp.int32, (count, count), 1
    )
    column = jnp.sum(jnp.where(here, values, 0.0), axis=1, keepdims=True)
    return jnp.broadcast_to(column, (count, TILE))


def spread(tile, live, first, count):
    groups = [jnp.where(tile == first + n, live, 0.0) for n in range(count)]
    return groups[0] if count == 1 else jnp.concatenate(groups, axis=1)


def padded(terms):
    return -(-terms // 16) * 16


def pair_factors(s, su, si, nu, ni, row_live, col_live, user_tiles, chunks):
    rows = row_live[s].astype(F32)
    cols = col_live[s].astype(F32)
    ones = jnp.ones((nu.shape[1], TILE), F32)
    at = slice(s, s + 1)
    spare = padded(su.shape[1] + nu.shape[1]) - su.shape[1] - nu.shape[1]
    left = jnp.concatenate(
        [
            spread(down(su[at, :]), rows, 0, user_tiles),
            spread(down(nu[at, :]), ones, 0, user_tiles),
            jnp.zeros((spare, user_tiles * TILE), F32),
        ],
        axis=0,
    )
    count = CHUNK // TILE
    item, sampled_item = down(si[at, :]), down(ni[at, :])
    rights = []
    for chunk in range(chunks):
        seen = spread(item, cols, chunk * count, count)
        sampled = spread(sampled_item, ones, chunk * count, count)
        rights.append(
            jnp.concatenate(
                [
                    jnp.concatenate([seen, seen], axis=1),
                    jnp.concatenate([NEG_WEIGHT * sampled, jnp.zeros_like(sampled)], axis=1),
                    jnp.zeros((spare, 2 * CHUNK), F32),
                ],
                axis=0,
            ).astype(BF)
        )
    return left.T.astype(BF), rights


def adagrad(factor, accum, grad):
    accum = accum + grad * grad
    return factor - LEARN_RATE * grad * lax.rsqrt(accum), accum


def dot(a, b, contract):
    return lax.dot_general(a, b, ((contract[:1], contract[1:]), ((), ())), preferred_element_type=F32)


def chunk_terms(users, left, right, factor, each):
    item_bf = factor.astype(BF)
    grad_items = DECAY * factor
    for start in range(0, users.shape[0], STEP):
        at = slice(start, start + STEP)
        user = users[at, :]
        user_bf = user.astype(BF)
        scores = dot(user_bf, item_bf, (1, 1))
        both = dot(left[at, :], right, (1, 0))
        err = (both[:, :CHUNK] * scores - both[:, CHUNK:]).astype(BF)
        each(at, user, dot(err, item_bf, (1, 0)))
        grad_items += dot(err, user_bf, (0, 0))
    return grad_items


def store_state(state, factor, accum):
    state[:CHUNK, :] = factor
    state[CHUNK:, :] = accum


def first_kernel(chunks, *refs):
    args, outs, scratch = refs[:10], refs[10 : 10 + 5 + chunks], refs[10 + 5 + chunks :]
    users_hbm, user_accum_hbm, items_hbm, item_accum_hbm = args[:4]
    users, user_accum, left_out, right_out, grad_out, *states = outs
    small, (raw, sems) = scratch[:6], scratch[6:]
    copies = []
    for n, (src, dst) in enumerate(zip(args[4:], small)):
        if len(src.shape) == 3:
            src, dst = src.at[pl.ds(0, 1)], dst.at[pl.ds(0, 1)]
        copies.append(pltpu.make_async_copy(src, dst, sems.at[n]))
    copies.append(pltpu.make_async_copy(users_hbm, users, sems.at[6]))
    at = 7
    tile = ORDERS[0][0]
    for chunk in (tile, *(n for n in range(chunks) if n != tile)):
        target = raw if chunk == tile else states[chunk]
        rows = pl.ds(chunk * CHUNK, CHUNK)
        for part, source in enumerate((items_hbm, item_accum_hbm)):
            copies.append(
                pltpu.make_async_copy(
                    source.at[rows], target.at[pl.ds(part * CHUNK, CHUNK)], sems.at[at]
                )
            )
            at += 1
    copies.append(pltpu.make_async_copy(user_accum_hbm, user_accum, sems.at[at]))
    for copy in copies:
        copy.start()
    for copy in copies[:6]:
        copy.wait()
    su, si, row_live, col_live, nu, ni = small
    left, rights = pair_factors(0, su, si, nu, ni, row_live, col_live, users.shape[0] // TILE, chunks)
    left_out[...] = left
    for chunk in range(chunks):
        right_out[chunk] = rights[chunk]
    for copy in copies[6:9]:
        copy.wait()
    factor, accum = raw[:CHUNK, :], raw[CHUNK:, :]

    def each(at, user, grad):
        grad_out[at, :] = grad

    grad_items = chunk_terms(users, left_out, rights[tile], factor, each)
    store_state(states[tile], *adagrad(factor, accum, grad_items))
    for copy in copies[9:]:
        copy.wait()


def run_first(args):
    users, user_accum, items, item_accum, *small = args
    width = users.shape[1]
    chunks = items.shape[0] // CHUNK
    terms = padded(small[0].shape[1] + small[4].shape[1])
    sds = jax.ShapeDtypeStruct
    out = [
        sds(users.shape, F32),
        sds(users.shape, F32),
        sds((users.shape[0], terms), BF),
        sds((chunks, terms, 2 * CHUNK), BF),
        sds(users.shape, F32),
    ] + [sds((2 * CHUNK, width), F32)] * chunks
    return pl.pallas_call(
        functools.partial(first_kernel, chunks),
        out_shape=out,
        in_specs=[HBM_SPEC] * len(args),
        out_specs=[VMEM_SPEC] * len(out),
        scratch_shapes=[pltpu.VMEM(x.shape, x.dtype) for x in small]
        + [pltpu.VMEM((2 * CHUNK, width), F32), pltpu.SemaphoreType.DMA((8 + 2 * chunks,))],
        compiler_params=PARAMS,
        name="first_chunk",
    )(*(pltpu.with_memory_space_constraint(x, pltpu.HBM) for x in args))


def factors_kernel(user_tiles, chunks, *refs):
    args, (left_out, right_out), (*small, sems) = refs[:6], refs[7:9], refs[9:]
    copies = [pltpu.make_async_copy(src, dst, sems.at[n]) for n, (src, dst) in enumerate(zip(args, small))]
    for copy in copies:
        copy.start()
    for copy in copies:
        copy.wait()
    su, si, row_live, col_live, nu, ni = small
    for s in range(1, SUBS):
        left, rights = pair_factors(s, su, si, nu, ni, row_live, col_live, user_tiles, chunks)
        left_out[s - 1] = left
        for chunk in range(chunks):
            right_out[s - 1, chunk] = rights[chunk]


def run_factors(small, user_rows, chunks, after):
    terms = padded(small[0].shape[1] + small[4].shape[1])
    pinned = [pltpu.with_memory_space_constraint(x, pltpu.HBM) for x in small]
    return pl.pallas_call(
        functools.partial(factors_kernel, user_rows // TILE, chunks),
        out_shape=[
            jax.ShapeDtypeStruct((SUBS - 1, user_rows, terms), BF),
            jax.ShapeDtypeStruct((SUBS - 1, chunks, terms, 2 * CHUNK), BF),
        ],
        in_specs=[HBM_SPEC] * 6 + [pl.BlockSpec(memory_space=pl.ANY)],
        out_specs=[VMEM_SPEC] * 2,
        scratch_shapes=[pltpu.VMEM(x.shape, x.dtype) for x in small] + [pltpu.SemaphoreType.DMA((6,))],
        compiler_params=PARAMS,
        name="pair_factors",
    )(*pinned, after)


def chunk_kernel(s, chunk, first, final, chunks, *refs):
    users, left, right, state, *refs = refs
    if s > 0:
        left, right = left.at[s - 1], right.at[s - 1]
    right = right[chunk]
    if not first:
        grad_in, *refs = refs
    if final:
        user_accum, *refs = refs
    end = final and s == SUBS - 1
    if end:
        others, refs = refs[: chunks - 1], refs[chunks - 1 :]
        outs, (users_out, user_accum_out, state_out, sems) = refs[:4], refs[4:]
        copies = []

        def send(src, dst):
            copies.append(pltpu.make_async_copy(src, dst, sems.at[len(copies)]))
            copies[-1].start()

        for n, other in zip([n for n in range(chunks) if n != chunk], others):
            for part in range(2):
                send(other.at[pl.ds(part * CHUNK, CHUNK)], outs[2 + part].at[pl.ds(n * CHUNK, CHUNK)])
    elif final:
        users_out, user_accum_out, state_out = refs
    else:
        grad_out, state_out = refs
    factor, accum = state[:CHUNK, :], state[CHUNK:, :]

    def each(at, user, grad):
        if not first:
            grad += grad_in[at, :]
        if final:
            grad += DECAY * user
            users_out[at, :], user_accum_out[at, :] = adagrad(user, user_accum[at, :], grad)
            if end:
                rows = pl.ds(at.start, STEP)
                send(users_out.at[rows], outs[0].at[rows])
                send(user_accum_out.at[rows], outs[1].at[rows])
        else:
            grad_out[at, :] = grad

    grad_items = chunk_terms(users, left, right, factor, each)
    store_state(state_out, *adagrad(factor, accum, grad_items))
    if end:
        for part in range(2):
            send(state_out.at[pl.ds(part * CHUNK, CHUNK)], outs[2 + part].at[pl.ds(chunk * CHUNK, CHUNK)])
        for copy in copies:
            copy.wait()


def run_chunk(s, chunk, first, final, chunks, users, factors, state, extra):
    width = users.shape[1]
    user_shape = jax.ShapeDtypeStruct(users.shape, F32)
    state_shape = jax.ShapeDtypeStruct((2 * CHUNK, width), F32)
    end = final and s == SUBS - 1
    out = [user_shape] * (2 if final else 1)
    out += [jax.ShapeDtypeStruct((chunks * CHUNK, width), F32)] * 2 if end else [state_shape]
    scratch = []
    if end:
        copies = 2 * chunks + 2 * (users.shape[0] // STEP)
        scratch = [pltpu.VMEM(x.shape, F32) for x in (users, users, state)]
        scratch.append(pltpu.SemaphoreType.DMA((copies,)))
    operands = [users, *factors, state, *extra]
    return pl.pallas_call(
        functools.partial(chunk_kernel, s, chunk, first, final, chunks),
        out_shape=out,
        in_specs=[VMEM_SPEC] * len(operands),
        out_specs=[HBM_SPEC if end else VMEM_SPEC] * len(out),
        scratch_shapes=scratch,
        compiler_params=PARAMS,
        cost_estimate=pl.CostEstimate(
            flops=10 * users.shape[0] * CHUNK * width, bytes_accessed=6 * 1024 * 1024, transcendentals=0
        ),
        name=f"sub{s}_chunk{chunk}",
    )(*operands)


def move(state, s, second_half):
    blks, xors = lax.axis_size("blk"), lax.axis_size("xor")
    flip = 2 ** (s % 2) if second_half else 0
    pairs = [
        (b * xors + x, ((b + 1) % blks) * xors + (x ^ flip)) for b in range(blks) for x in range(xors)
    ]
    return lax.ppermute(state, AXES, pairs)


def per_device(*args):
    chunks = args[2].shape[0] // CHUNK
    users, user_accum, left, right, grad, *states = run_first(args)
    factors = (left, right)
    grad = [grad]
    for s, order in enumerate(ORDERS):
        moved = [None] * chunks
        for n in order:
            first, final = n == order[0], n == order[-1]
            extra = (*grad, user_accum) if final else grad
            end = s == SUBS - 1
            if final and end:
                extra = (*extra, *(m for m in moved if m is not None))
                return tuple(run_chunk(s, n, first, final, chunks, users, factors, states[n], extra))
            state = states[n]
            if s > 0 or not first:
                *grad, state = run_chunk(s, n, first, final, chunks, users, factors, state, extra)
            moved[n] = state if end else move(state, s, n >= chunks // 2)
        users, user_accum = grad
        grad = []
        states = moved
        if s == 0:
            factors = run_factors(args[4:], users.shape[0], chunks, users)


def solution(mesh):
    rows = P(AXES, None)
    placed = (rows,) * 4 + (P(None, AXES),) * 2 + (P(None, AXES, None),) * 2 + (P(None, AXES),) * 2
    return jax.shard_map(
        per_device, mesh=mesh, in_specs=placed, out_specs=(rows,) * 4, check_vma=False
    )
```
